32 devices in a mesh: lat: 4 (over x, core), tm: 8 (over z, y).
Axes of the slice: x: 2, y: 2, z: 4, core: 2. Of those that a mesh axis runs over, the one named last changes fastest.
Arguments:
- data: float32 [8, 128, 23040], P(None, 'tm', 'lat'), may hold values from -6 to 6
- space_init: float32 [32, 23040], P(None, 'lat'), may hold values from -0.0390625 to 0.0390625
- time_init: float32 [32, 128], P(None, 'tm'), may hold values from -6 to 6
- variable_factor: float32 [8, 32], replicated, may hold values from -2 to 2
- neighbours: int32 [4, 23040], P(None, 'lat'), may hold values from -1 to 23039, as said below
Outputs:
- time_factor: float32 [32, 128], P(None, 'tm')
- space_factor: float32 [32, 23040], P(None, 'lat')
The draws below stay inside these ranges and needn't reach their ends.
Inputs may be any that keep to these rules, and one draw needn't show every extreme that they name: `neighbours`: points are numbered row by row: latitude row i holds points i * 360 to (i + 1) * 360 - 1. Rows 0 and 1 name the east and west neighbour in the same latitude row (cyclic in longitude); rows 2 and 3 name a point of the latitude row before and after, at most one column away (cyclic); -1 where the grid has no such row.
All inputs are finite; a program needn't handle non-finite values.
Results may differ from the reference program's by a relative error of at most 0.0001.
Values sent between devices are 32-bit elements; how exact they have to be, the bound alone decides.
A program may use at most 64 MiB of HBM per device.

```python
import jax
import jax.numpy as jnp
from jax import lax

VARS = 8
RANK = 32
NLON = 360
SWEEPS = 8
NLAT = 64
POINTS = 23040
HOURS = 128


def draw_neighbours(key, part):
    offsets = jax.random.randint(jax.random.fold_in(key, 17), (2, POINTS), -1, 2)
    positions = jnp.arange(POINTS, dtype=jnp.int32)
    row_index = positions // NLON
    column = positions % NLON
    east = row_index * NLON + (column + 1) % NLON
    west = row_index * NLON + (column - 1 + NLON) % NLON
    north = jnp.where(row_index > 0, (row_index - 1) * NLON + (column + offsets[0] + NLON) % NLON, -1)
    south = jnp.where(row_index < NLAT - 1, (row_index + 1) * NLON + (column + offsets[1] + NLON) % NLON, -1)
    return jnp.stack([east, west, north, south]).astype(jnp.int32)


def levels(rng, dims, pieces, least, high):
    def one(position, parts):
        draws = jax.random.uniform(jax.random.fold_in(jax.random.fold_in(rng, 6), position), (parts,), jnp.float32, least / len(pieces), high / len(pieces))
        return jnp.repeat(jnp.exp(draws), dims[position] // parts).reshape((-1,) + (1,) * (len(dims) - position - 1))

    gain = one(*pieces[0])
    for cut in pieces[1:]:
        gain = gain * one(*cut)
    return gain


def normal_values(rng, dims, spread, bound, pieces=(), kind=jnp.bfloat16):
    values = spread * jax.random.normal(rng, dims, jnp.float32)
    if pieces:
        values = values * levels(rng, dims, pieces, -0.22, 0.18)
    return jnp.clip(values, -bound, bound).astype(kind)


def setup_inputs(seed: int = 0) -> dict:
    keys = jax.random.split(jax.random.key(seed), 6)
    data = normal_values(keys[0], (VARS, HOURS, POINTS), 1.0, 6.0, ((1, 8), (2, 4)), jnp.float32)
    space_init = normal_values(keys[1], (RANK, POINTS), POINTS ** -0.5, 0.0390625, ((1, 4),), jnp.float32)
    time_init = normal_values(keys[2], (RANK, HOURS), 1.0, 6.0, ((1, 8),), jnp.float32)
    variable_factor = normal_values(keys[3], (VARS, RANK), VARS ** -0.5, 2.0, (), jnp.float32)
    neighbours = draw_neighbours(jax.random.fold_in(keys[5], 71), 0)
    return {"data": data, "space_init": space_init, "time_init": time_init, "variable_factor": variable_factor, "neighbours": neighbours}


def inverse(matrix):
    lower = jnp.linalg.cholesky(matrix)
    identity = jnp.eye(matrix.shape[0], dtype=jnp.float32)
    return jax.scipy.linalg.cho_solve((lower, True), identity)

def reference(data, space_init, time_init, variable_factor, neighbours):
    highest = lax.Precision.HIGHEST
    var_count, hour_count, point_count = data.shape
    rank_count = space_init.shape[0]
    identity = jnp.eye(rank_count, dtype=jnp.float32)
    unfolded = data.reshape(var_count * hour_count, point_count)
    var_gram = jnp.dot(variable_factor.T.astype(jnp.float32), variable_factor.astype(jnp.float32), precision=highest, preferred_element_type=jnp.float32)
    space_gram = lax.dot_general(space_init.astype(jnp.float32), space_init.astype(jnp.float32), (((1,), (1,)), ((), ())), precision=highest, preferred_element_type=jnp.float32)
    projected = lax.dot_general(space_init.astype(jnp.float32), unfolded.astype(jnp.float32), (((1,), (1,)), ((), ())), precision=highest, preferred_element_type=jnp.float32)
    projected = projected.reshape(rank_count, var_count, hour_count)
    time_rhs = lax.optimization_barrier(jnp.sum(projected * variable_factor.T[:, :, None], axis=1))
    padded = jnp.pad(time_init, ((0, 0), (2, 2)))
    stencil = padded[:, :-4] - 4.0 * padded[:, 1:-3] - 4.0 * padded[:, 3:-1] + padded[:, 4:]
    time_inv = inverse(space_gram * var_gram + 3.0 * identity)
    time_factor = jnp.dot(time_inv.astype(jnp.float32), (time_rhs - 0.5 * stencil).astype(jnp.float32), precision=highest, preferred_element_type=jnp.float32)
    time_gram = lax.dot_general(time_factor.astype(jnp.float32), time_factor.astype(jnp.float32), (((1,), (1,)), ((), ())), precision=highest, preferred_element_type=jnp.float32)
    scale = jnp.sqrt(jnp.diagonal(time_gram) + 1e-06)
    point_op = time_gram / (scale[:, None] * scale[None, :]) * var_gram + 2.0 * identity
    point_inv = inverse(point_op)
    weighted = (variable_factor.T[:, :, None] * time_factor[:, None, :]).reshape(rank_count, var_count * hour_count)
    point_rhs = jnp.dot(weighted.astype(jnp.float32), unfolded.astype(jnp.float32), precision=highest, preferred_element_type=jnp.float32) / scale[:, None]
    valid = neighbours >= 0
    clipped = jnp.maximum(neighbours, 0).reshape(-1)
    current = space_init
    for sweep_index in range(SWEEPS):
        near = jnp.take(current, clipped, axis=1).reshape(rank_count, 4, point_count)
        near_sum = lax.optimization_barrier(jnp.sum(jnp.where(valid[None], near, jnp.float32(0.0)), axis=1))
        current = jnp.dot(point_inv.astype(jnp.float32), (point_rhs + 0.5 * near_sum).astype(jnp.float32), precision=highest, preferred_element_type=jnp.float32)
    return (time_factor, current)
```

```python
import functools

import jax
import jax.numpy as jnp
import numpy as np
from jax import lax
from jax.experimental import pallas as pl
from jax.experimental.pallas import tpu as pltpu
from jax.sharding import PartitionSpec as P

NLON = 360
SWEEPS = 8
WIDE = 384
SIDE = (WIDE - NLON) // 2
WINDOW = 512
F32 = jnp.float32
BF16 = jnp.bfloat16
HIGHEST = lax.Precision.HIGHEST
MESH = pl.DeviceIdType.MESH
NN = (((1,), (0,)), ((), ()))
NT = (((1,), (1,)), ((), ()))
TN = (((0,), (0,)), ((), ()))


def exact_dot(a, b, dims=NN):
    return lax.dot_general(a, b, dims, precision=HIGHEST, preferred_element_type=F32)


def halves(x):
    high = x.astype(BF16)
    return high, (x - high.astype(F32)).astype(BF16)


def left_stack(x):
    high, low = halves(x)
    return jnp.concatenate([high, high, low], axis=1)


def split_dot(stack, b):
    high, low = halves(b)
    return jnp.dot(stack, jnp.concatenate([high, low, high], axis=0), preferred_element_type=F32)


def inverse(matrix, row_id, col_id):
    for k in range(matrix.shape[0]):
        pivot = 1.0 / matrix[k : k + 1, k : k + 1]
        row = jnp.where(col_id[:1] == k, 1.0, matrix[k : k + 1, :]) * pivot
        rest = jnp.where(col_id == k, 0.0, matrix) - matrix[:, k : k + 1] * row
        matrix = jnp.where(row_id == k, row, rest)
    return matrix


def window_of(row, total):
    start = min(row * NLON // 128 * 128, total - WINDOW)
    return start, row * NLON - start


def spread_row(load, row, total, lane):
    start, shift = window_of(row, total)
    cells = load(start)
    if shift:
        cells = pltpu.roll(cells, WINDOW - shift, 1)
    cells = cells[:, :WIDE]
    after = pltpu.roll(cells, NLON, 1)
    before = pltpu.roll(cells, WIDE - NLON, 1)
    return jnp.where(lane < NLON, cells, jnp.where(lane < NLON + SIDE, after, before))


def kernel(
    lats, tms, data_ref, space_ref, time_ref, var_ref, links_ref, expand_ref, tile_ref, taps_ref,
    time_out, space_out,
    small, small_in, edge, edge_in, gram, gram_in, flat, terms, terms_in, rhs, codes,
    centre, east, west,
    small_s, small_r, edge_s, edge_r, halo_s, halo_r, gram_s, gram_r, rs_s, rs_r, ag_s, ag_r, fw_s, fw_r,
):
    lat, tm = lax.axis_index("lat"), lax.axis_index("tm")
    rank, points = space_ref.shape
    hours = time_ref.shape[1]
    rows = points // NLON
    deep = SWEEPS
    extent = rows + 2 * deep
    share = rows // tms
    north, south = lat > 0, lat < lats - 1

    def to_lat(offset):
        return {"lat": lax.rem(lat + offset, lats)}

    def to_tm(offset):
        return {"tm": lax.rem(tm + offset, tms)}

    def send(src, dst, send_sem, recv_sem, device):
        return pltpu.make_async_remote_copy(
            src_ref=src, dst_ref=dst, send_sem=send_sem, recv_sem=recv_sem,
            device_id=device, device_id_type=MESH,
        )

    barrier = pltpu.get_barrier_semaphore()
    for d in range(1, lats):
        pl.semaphore_signal(barrier, inc=1, device_id=to_lat(d), device_id_type=MESH)
    for d in range(1, tms):
        pl.semaphore_signal(barrier, inc=1, device_id=to_tm(d), device_id_type=MESH)

    edge[...] = jnp.zeros_like(edge)
    edge[:, :hours] = time_ref[...]
    pl.semaphore_wait(barrier, lats + tms - 2)
    up = send(edge, edge_in.at[0], edge_s.at[0], edge_r.at[0], to_tm(1))
    down = send(edge, edge_in.at[1], edge_s.at[1], edge_r.at[1], to_tm(tms - 1))
    up.start()
    down.start()

    chunk = points // 5

    def gather(i, sums):
        cells = pl.ds(pl.multiple_of(i * chunk, 128), chunk)
        mine = space_ref[:, cells]
        return (
            sums[0] + exact_dot(mine, data_ref[:, cells], NT),
            sums[1] + exact_dot(mine, mine, NT),
        )

    projected, local_gram = lax.fori_loop(
        0, 5, gather,
        (jnp.zeros((rank, data_ref.shape[0]), F32), jnp.zeros((rank, rank), F32)),
    )
    weights = exact_dot(var_ref[...], expand_ref[...], TN)
    small[...] = jnp.zeros_like(small)
    small[0, :, :rank] = local_gram
    small[1, :, :hours] = exact_dot(projected * weights, tile_ref[...], NT)
    small_sends = []
    for d in range(1, lats):
        copy = send(small, small_in.at[d], small_s.at[d], small_r.at[d], to_lat(d))
        copy.start()
        small_sends.append(copy)

    lane = lax.broadcasted_iota(jnp.int32, (rank, WIDE), 1)
    place = lax.broadcasted_iota(jnp.int32, (1, points), 1) + lat * points
    for side, step in ((0, -NLON), (1, NLON)):
        link = links_ref[2 + side : 3 + side, :]
        shift = link - (place + step)
        ahead = (shift == 1) | (shift == 1 - NLON)
        behind = (shift == -1) | (shift == NLON - 1)
        code = jnp.where(link < 0, 3.0, jnp.where(ahead, 1.0, jnp.where(behind, 2.0, 0.0)))
        flat[0:8, :] = jnp.broadcast_to(code, (8, points))
        for row in range(rows):
            codes[deep + row, side] = spread_row(
                lambda s: flat[0:8, s : s + WINDOW], row, points, lane[:8]
            )
    for row in range(rows):
        centre[0, deep + row] = spread_row(
            lambda s: space_ref[:, s : s + WINDOW], row, points, lane
        )
    top, bottom = pl.ds(deep, deep), pl.ds(rows, deep)
    before, behind_rows = pl.ds(0, deep), pl.ds(rows + deep, deep)
    halo = []
    for side, (exists, mine, theirs, offset) in enumerate(
        ((north, top, behind_rows, lats - 1), (south, bottom, before, 1))
    ):
        a = send(centre.at[0, mine], centre.at[0, theirs], halo_s.at[side, 0], halo_r.at[side, 0], to_lat(offset))
        b = send(codes.at[mine], codes.at[theirs], halo_s.at[side, 1], halo_r.at[side, 1], to_lat(offset))
        halo.append((exists, a, b))

        @pl.when(exists)
        def _(a=a, b=b):
            a.start()
            b.start()

    row_id = lax.broadcasted_iota(jnp.int32, (rank, rank), 0)
    col_id = lax.broadcasted_iota(jnp.int32, (rank, rank), 1)
    eye = jnp.where(row_id == col_id, F32(1.0), F32(0.0))
    var_gram = exact_dot(var_ref[...], var_ref[...], TN)
    up.wait()
    down.wait()
    past = jnp.where(tm > 0, edge_in[0, :, :hours], 0.0)
    coming = jnp.where(tm < tms - 1, edge_in[1, :, :hours], 0.0)
    stencil = (
        exact_dot(past, taps_ref[0]) + exact_dot(time_ref[...], taps_ref[1]) + exact_dot(coming, taps_ref[2])
    )
    total = small[...]
    for d, copy in enumerate(small_sends, 1):
        copy.wait()
        total = total + small_in[d]
    space_gram, time_rhs = total[0, :, :rank], total[1, :, :hours]
    time_inv = inverse(space_gram * var_gram + 3.0 * eye, row_id, col_id)
    time_factor = exact_dot(time_inv, time_rhs - 0.5 * stencil)
    time_out[...] = time_factor
    gram[...] = jnp.zeros_like(gram)
    gram[:, :rank] = exact_dot(time_factor, time_factor, NT)
    gram_sends = []
    for d in range(1, tms):
        copy = send(gram, gram_in.at[d], gram_s.at[d], gram_r.at[d], to_tm(d))
        copy.start()
        gram_sends.append(copy)

    stack = left_stack(weights * exact_dot(time_factor, tile_ref[...]))

    @pl.loop(0, 5)
    def _(i):
        cells = pl.ds(pl.multiple_of(i * chunk, 128), chunk)
        flat[:, cells] = split_dot(stack, data_ref[:, cells])

    for row in range(rows):
        terms[row] = spread_row(lambda s: flat[:, s : s + WINDOW], row, points, lane)
    rs_sends = []
    for d in range(1, tms):
        target = lax.rem(tm + d, tms)
        copy = send(terms.at[pl.ds(target * share, share)], terms_in.at[d], rs_s.at[d], rs_r.at[d], to_tm(d))
        copy.start()
        rs_sends.append(copy)

    time_gram = gram[:, :rank]
    for d, copy in enumerate(gram_sends, 1):
        copy.wait()
        time_gram = time_gram + gram_in[d, :, :rank]
    diagonal = time_gram * eye
    scale = jnp.sqrt(jnp.sum(diagonal, axis=1, keepdims=True) + 1e-06)
    scale_row = jnp.sqrt(jnp.sum(diagonal, axis=0, keepdims=True) + 1e-06)
    point_inv = inverse(time_gram / (scale * scale_row) * var_gram + 2.0 * eye, row_id, col_id)
    sweep_stack = left_stack(point_inv)

    mine = pl.ds(tm * share, share)
    owned = terms[mine]
    for d, copy in enumerate(rs_sends, 1):
        copy.wait_recv()
        owned = owned + terms_in[d]
    held = pl.ds(deep + tm * share, share)
    rhs[held] = owned / scale[None]
    ag_sends = []
    for d in range(1, tms):
        copy = send(rhs.at[held], rhs.at[held], ag_s.at[d], ag_r.at[d], to_tm(d))
        copy.start()
        ag_sends.append(copy)

    def shift_row(buf, row):
        cells = centre[buf, row]
        east[buf, row] = pltpu.roll(cells, WIDE - 1, 1)
        west[buf, row] = pltpu.roll(cells, 1, 1)

    for side, arrives in ((0, south), (1, north)):
        _, a, b = halo[side]

        @pl.when(arrives)
        def _(a=a, b=b):
            a.wait_recv()
            b.wait_recv()

    for exists, a, b in halo:

        @pl.when(exists)
        def _(a=a, b=b):
            a.wait_send()
            b.wait_send()

    @pl.loop(0, extent)
    def _(row):
        shift_row(0, row)

    def forward(source, start):
        block = source * share
        for side, exists, wanted, offset, move in (
            (0, north, block < deep, lats - 1, rows),
            (1, south, block + share > rows - deep, 1, -rows),
        ):
            place = deep + block + jnp.where(wanted, move, 0)
            copy = send(
                rhs.at[pl.ds(deep + block, share)], rhs.at[pl.ds(place, share)],
                fw_s.at[side, source], fw_r.at[side, source], to_lat(offset),
            )

            @pl.when(jnp.logical_and(exists, wanted))
            def _():
                if start:
                    copy.start()
                else:
                    copy.wait_send()

    forward(tm, True)
    for d, copy in enumerate(ag_sends, 1):
        copy.wait_recv()
        forward(lax.rem(tm + tms - d, tms), True)

    for side, arrives in ((0, south), (1, north)):
        for source in range(tms):
            block = source * share
            if (block < deep) if side == 0 else (block + share > rows - deep):
                move = rows if side == 0 else -rows
                copy = send(
                    rhs.at[pl.ds(deep + block, share)], rhs.at[pl.ds(deep + block + move, share)],
                    fw_s.at[side, source], fw_r.at[side, source], to_lat(1),
                )

                @pl.when(arrives)
                def _(copy=copy):
                    copy.wait_recv()

    def pick(buf, row, code):
        a = centre[buf, row].reshape(rank // 8, 8, WIDE)
        e = east[buf, row].reshape(rank // 8, 8, WIDE)
        w = west[buf, row].reshape(rank // 8, 8, WIDE)
        code = code[None]
        moved = jnp.where(code == 1.0, e, jnp.where(code == 2.0, w, a))
        return jnp.where(code == 3.0, 0.0, moved)

    for sweep in range(SWEEPS):
        now, later = sweep % 2, (sweep + 1) % 2
        least = sweep + 1

        def one(row, now=now, later=later, sweep=sweep):
            sides = (east[now, row] + west[now, row]).reshape(rank // 8, 8, WIDE)
            near = sides + pick(now, row - 1, codes[row, 0]) + pick(now, row + 1, codes[row, 1])
            cells = split_dot(sweep_stack, rhs[row] + 0.5 * near.reshape(rank, WIDE))
            centre[later, row] = cells
            if sweep < SWEEPS - 1:
                east[later, row] = pltpu.roll(cells, WIDE - 1, 1)
                west[later, row] = pltpu.roll(cells, 1, 1)

        @pl.loop(0, (extent - 2 * least) // 2)
        def _(i, one=one, least=least):
            one(least + 2 * i)
            one(least + 2 * i + 1)

    last = SWEEPS % 2
    wide_lane = lax.broadcasted_iota(jnp.int32, (rank, WINDOW), 1)
    for row in range(rows):
        start, shift = window_of(row, points)
        cells = jnp.concatenate([centre[last, deep + row], jnp.zeros((rank, WINDOW - WIDE), F32)], axis=1)
        if shift:
            cells = pltpu.roll(cells, shift, 1)
        inside = (wide_lane >= shift) & (wide_lane < shift + NLON)
        old = space_out[:, start : start + WINDOW]
        space_out[:, start : start + WINDOW] = jnp.where(inside, cells, old)

    for copy in rs_sends + ag_sends:
        copy.wait_send()
    for source in range(tms):
        forward(jnp.int32(source), False)


def per_device(lats, tms, data, space_init, time_init, variable_factor, neighbours):
    var_count, hours, points = data.shape
    rank = space_init.shape[0]
    rows = points // NLON
    extent = rows + 2 * SWEEPS
    share = rows // tms
    columns = np.arange(var_count * hours)
    expand = (columns[None] // hours == np.arange(var_count)[:, None]).astype(np.float32)
    tile = (columns[None] % hours == np.arange(hours)[:, None]).astype(np.float32)
    wide = np.zeros((3 * hours, hours), np.float32)
    for h in range(hours):
        for step, tap in ((-2, 1.0), (-1, -4.0), (1, -4.0), (2, 1.0)):
            wide[hours + h + step, h] = tap
    taps = wide.reshape(3, hours, hours)
    vmem = pl.BlockSpec(memory_space=pltpu.VMEM)
    dma = pltpu.SemaphoreType.DMA
    return pl.pallas_call(
        functools.partial(kernel, lats, tms),
        out_shape=(
            jax.ShapeDtypeStruct((rank, hours), F32),
            jax.ShapeDtypeStruct((rank, points), F32),
        ),
        in_specs=[vmem] * 8,
        out_specs=(vmem, vmem),
        scratch_shapes=[
            pltpu.VMEM((2, rank, 128), F32),
            pltpu.VMEM((lats, 2, rank, 128), F32),
            pltpu.VMEM((rank, 128), F32),
            pltpu.VMEM((2, rank, 128), F32),
            pltpu.VMEM((rank, 128), F32),
            pltpu.VMEM((tms, rank, 128), F32),
            pltpu.VMEM((rank, points), F32),
            pltpu.VMEM((rows, rank, WIDE), F32),
            pltpu.VMEM((tms, share, rank, WIDE), F32),
            pltpu.VMEM((extent, rank, WIDE), F32),
            pltpu.VMEM((extent, 2, 8, WIDE), F32),
            pltpu.VMEM((2, extent, rank, WIDE), F32),
            pltpu.VMEM((2, extent, rank, WIDE), F32),
            pltpu.VMEM((2, extent, rank, WIDE), F32),
            dma((lats,)), dma((lats,)), dma((2,)), dma((2,)), dma((2, 2)), dma((2, 2)),
            dma((tms,)), dma((tms,)), dma((tms,)), dma((tms,)), dma((tms,)), dma((tms,)),
            dma((2, tms)), dma((2, tms)),
        ],
        compiler_params=pltpu.CompilerParams(
            collective_id=0, has_side_effects=True, vmem_limit_bytes=56 * 2**20
        ),
    )(
        data.reshape(var_count * hours, points), space_init, time_init, variable_factor, neighbours,
        jnp.asarray(expand), jnp.asarray(tile), jnp.asarray(taps),
    )


def solution(mesh):
    placed = (P(None, "tm", "lat"), P(None, "lat"), P(None, "tm"), P(), P(None, "lat"))
    return jax.shard_map(
        functools.partial(per_device, mesh.shape["lat"], mesh.shape["tm"]),
        mesh=mesh,
        in_specs=placed,
        out_specs=(P(None, "tm"), P(None, "lat")),
        check_vma=False,
    )
```

```python
import functools

import jax
import jax.numpy as jnp
import numpy as np
from jax import lax
from jax.experimental import pallas as pl
from jax.experimental.pallas import tpu as pltpu
from jax.sharding import PartitionSpec as P

NLON = 360
SWEEPS = 8
WIDE = 384
SIDE = (WIDE - NLON) // 2
WINDOW = 512
BATCH = 8
F32 = jnp.float32
BF16 = jnp.bfloat16
HIGHEST = lax.Precision.HIGHEST
MESH = pl.DeviceIdType.MESH
NN = (((1,), (0,)), ((), ()))
NT = (((1,), (1,)), ((), ()))
TN = (((0,), (0,)), ((), ()))


def exact_dot(a, b, dims=NN):
    return lax.dot_general(a, b, dims, precision=HIGHEST, preferred_element_type=F32)


def halves(x):
    high = x.astype(BF16)
    return high, (x - high.astype(F32)).astype(BF16)


def left_stack(x):
    high, low = halves(x)
    return jnp.concatenate([high, high, low], axis=1)


def split_dot(stack, b):
    high, low = halves(b)
    return jnp.dot(stack, jnp.concatenate([high, low, high], axis=0), preferred_element_type=F32)


def inverse(matrix, row_id, col_id):
    for k in range(matrix.shape[0]):
        pivot = 1.0 / matrix[k : k + 1, k : k + 1]
        row = jnp.where(col_id[:1] == k, 1.0, matrix[k : k + 1, :]) * pivot
        rest = jnp.where(col_id == k, 0.0, matrix) - matrix[:, k : k + 1] * row
        matrix = jnp.where(row_id == k, row, rest)
    return matrix


def window_of(row, total):
    start = min(row * NLON // 128 * 128, total - WINDOW)
    return start, row * NLON - start


def spread_row(load, row, total, lane):
    start, shift = window_of(row, total)
    cells = load(start)
    if shift:
        cells = pltpu.roll(cells, WINDOW - shift, 1)
    cells = cells[:, :WIDE]
    after = pltpu.roll(cells, NLON, 1)
    before = pltpu.roll(cells, WIDE - NLON, 1)
    return jnp.where(lane < NLON, cells, jnp.where(lane < NLON + SIDE, after, before))


def kernel(
    lats, tms, data_ref, space_ref, time_ref, var_ref, links_ref, expand_ref, tile_ref, taps_ref,
    time_out, space_out,
    small, small_in, edge, edge_in, gram, gram_in, flat, terms, terms_in, rhs, codes,
    centre, east, west, centre_b, east_b, west_b,
    small_s, small_r, edge_s, edge_r, halo_s, halo_r, gram_s, gram_r, rs_s, rs_r, ag_s, ag_r, fw_s, fw_r,
    pair_in, partial, pair_s, pair_r, cross_s, cross_r,
):
    lat, tm = lax.axis_index("lat"), lax.axis_index("tm")
    rank, points = space_ref.shape
    hours = time_ref.shape[0]
    rows = points // NLON
    deep = SWEEPS
    extent = rows + 2 * deep
    share = rows // tms
    north, south = lat > 0, lat < lats - 1
    factors = ((centre, east, west), (centre_b, east_b, west_b))

    def to_lat(offset):
        return {"lat": lax.rem(lat + offset, lats)}

    def to_tm(offset):
        return {"tm": lax.rem(tm + offset, tms)}

    def send(src, dst, send_sem, recv_sem, device):
        return pltpu.make_async_remote_copy(
            src_ref=src, dst_ref=dst, send_sem=send_sem, recv_sem=recv_sem,
            device_id=device, device_id_type=MESH,
        )

    barrier = pltpu.get_barrier_semaphore()
    for d in range(1, lats):
        pl.semaphore_signal(barrier, inc=1, device_id=to_lat(d), device_id_type=MESH)
    for d in range(1, tms):
        pl.semaphore_signal(barrier, inc=1, device_id=to_tm(d), device_id_type=MESH)

    edge[...] = jnp.zeros_like(edge)
    edge[:, :rank] = time_ref[...]
    pl.semaphore_wait(barrier, lats + tms - 2)
    up = send(edge, edge_in.at[0], edge_s.at[0], edge_r.at[0], to_tm(1))
    down = send(edge, edge_in.at[1], edge_s.at[1], edge_r.at[1], to_tm(tms - 1))
    up.start()
    down.start()

    chunk = points // 5

    def gather(i, sums):
        cells = pl.ds(pl.multiple_of(i * chunk, 128), chunk)
        mine = space_ref[:, cells]
        return (
            sums[0] + exact_dot(mine, data_ref[:, cells], NT),
            sums[1] + exact_dot(mine, mine, NT),
        )

    projected, local_gram = lax.fori_loop(
        0, 5, gather,
        (jnp.zeros((rank, data_ref.shape[0]), F32), jnp.zeros((rank, rank), F32)),
    )
    weights = exact_dot(var_ref[...], expand_ref[...], TN)
    small[...] = jnp.zeros_like(small)
    small[0, :, :rank] = local_gram
    small[1, :, :hours] = exact_dot(projected * weights, tile_ref[...], NT)
    small_sends = []
    for d in range(1, lats):
        copy = send(small, small_in.at[d], small_s.at[d], small_r.at[d], to_lat(d))
        copy.start()
        small_sends.append(copy)

    lane = lax.broadcasted_iota(jnp.int32, (rank, WIDE), 1)
    place = lax.broadcasted_iota(jnp.int32, (1, points), 1) + lat * points
    for side, step in ((0, -NLON), (1, NLON)):
        link = links_ref[2 + side : 3 + side, :]
        shift = link - (place + step)
        ahead = (shift == 1) | (shift == 1 - NLON)
        behind = (shift == -1) | (shift == NLON - 1)
        code = jnp.where(link < 0, 3.0, jnp.where(ahead, 1.0, jnp.where(behind, 2.0, 0.0)))
        flat[0:8, :] = jnp.broadcast_to(code, (8, points))
        for row in range(rows):
            codes[deep + row, side] = spread_row(
                lambda s: flat[0:8, s : s + WINDOW], row, points, lane[:8]
            )
    for row in range(rows):
        centre[deep + row] = spread_row(
            lambda s: space_ref[:, s : s + WINDOW], row, points, lane
        )
    top, bottom = pl.ds(deep, deep), pl.ds(rows, deep)
    before, behind_rows = pl.ds(0, deep), pl.ds(rows + deep, deep)
    halo = []
    for side, (exists, mine, theirs, offset) in enumerate(
        ((north, top, behind_rows, lats - 1), (south, bottom, before, 1))
    ):
        a = send(centre.at[mine], centre.at[theirs], halo_s.at[side, 0], halo_r.at[side, 0], to_lat(offset))
        b = send(codes.at[mine], codes.at[theirs], halo_s.at[side, 1], halo_r.at[side, 1], to_lat(offset))
        halo.append((exists, a, b))

        @pl.when(exists)
        def _(a=a, b=b):
            a.start()
            b.start()

    row_id = lax.broadcasted_iota(jnp.int32, (rank, rank), 0)
    col_id = lax.broadcasted_iota(jnp.int32, (rank, rank), 1)
    eye = jnp.where(row_id == col_id, F32(1.0), F32(0.0))
    var_gram = exact_dot(var_ref[...], var_ref[...], TN)
    up.wait()
    down.wait()
    past = jnp.where(tm > 0, edge_in[0, :, :rank], 0.0)
    coming = jnp.where(tm < tms - 1, edge_in[1, :, :rank], 0.0)
    stencil = (
        exact_dot(past, taps_ref[0], TN)
        + exact_dot(time_ref[...], taps_ref[1], TN)
        + exact_dot(coming, taps_ref[2], TN)
    )
    total = small[...]
    for d, copy in enumerate(small_sends, 1):
        copy.wait()
        total = total + small_in[d]
    space_gram, time_rhs = total[0, :, :rank], total[1, :, :hours]
    time_inv = inverse(space_gram * var_gram + 3.0 * eye, row_id, col_id)
    time_factor = exact_dot(time_inv, time_rhs - 0.5 * stencil)
    time_out[...] = exact_dot(time_factor, eye, TN)
    gram[...] = jnp.zeros_like(gram)
    gram[:, :rank] = exact_dot(time_factor, time_factor, NT)
    gram_sends = []
    for d in range(1, tms):
        copy = send(gram, gram_in.at[d], gram_s.at[d], gram_r.at[d], to_tm(d))
        copy.start()
        gram_sends.append(copy)

    stack = left_stack(weights * exact_dot(time_factor, tile_ref[...]))

    @pl.loop(0, 5)
    def _(i):
        cells = pl.ds(pl.multiple_of(i * chunk, 128), chunk)
        flat[:, cells] = split_dot(stack, data_ref[:, cells])

    for row in range(rows):
        terms[row] = spread_row(lambda s: flat[:, s : s + WINDOW], row, points, lane)
    pairs = tms // 2
    low = lax.rem(tm, 2)
    other = {"tm": tm + 1 - 2 * low}

    def block_of(k, side):
        return lax.rem(tm // 2 + k, pairs) * 2 + side

    order = [*range(1, pairs), 0]
    pair_sends = {}
    for k in order:
        block = pl.ds(block_of(k, 1 - low) * share, share)
        pair_sends[k] = send(terms.at[block], pair_in.at[k], pair_s.at[k], pair_r.at[k], other)
        pair_sends[k].start()
    rs_sends = []
    for k in range(1, pairs):
        pair_sends[k].wait_recv()
        partial[k] = terms[pl.ds(block_of(k, low) * share, share)] + pair_in[k]
        copy = send(partial.at[k], terms_in.at[k], rs_s.at[k], rs_r.at[k], to_tm(2 * k))
        copy.start()
        rs_sends.append(copy)

    time_gram = gram[:, :rank]
    for d, copy in enumerate(gram_sends, 1):
        copy.wait()
        time_gram = time_gram + gram_in[d, :, :rank]
    diagonal = time_gram * eye
    scale = jnp.sqrt(jnp.sum(diagonal, axis=1, keepdims=True) + 1e-06)
    scale_row = jnp.sqrt(jnp.sum(diagonal, axis=0, keepdims=True) + 1e-06)
    point_inv = inverse(time_gram / (scale * scale_row) * var_gram + 2.0 * eye, row_id, col_id)
    sweep_stack = left_stack(point_inv)

    mine = pl.ds(tm * share, share)
    pair_sends[0].wait_recv()
    owned = terms[mine] + pair_in[0]
    for d, copy in enumerate(rs_sends, 1):
        copy.wait_recv()
        owned = owned + terms_in[d]
    held = pl.ds(deep + tm * share, share)
    rhs[held] = owned / scale[None]
    ag_sends = []
    for k in range(1, pairs):
        copy = send(rhs.at[held], rhs.at[held], ag_s.at[k], ag_r.at[k], to_tm(2 * k))
        copy.start()
        ag_sends.append(copy)

    def across(k):
        block = pl.ds(deep + block_of(pairs - k, low) * share, share)
        copy = send(rhs.at[block], rhs.at[block], cross_s.at[k], cross_r.at[k], other)
        copy.start()
        return copy

    cross_sends = [across(0)]

    for side, arrives in ((0, south), (1, north)):
        _, a, b = halo[side]

        @pl.when(arrives)
        def _(a=a, b=b):
            a.wait_recv()
            b.wait_recv()

    for exists, a, b in halo:

        @pl.when(exists)
        def _(a=a, b=b):
            a.wait_send()
            b.wait_send()

    @pl.loop(0, extent)
    def _(row):
        cells = centre[row]
        east[row] = pltpu.roll(cells, WIDE - 1, 1)
        west[row] = pltpu.roll(cells, 1, 1)

    def forward(source, start):
        block = source * share
        for side, exists, wanted, offset, move in (
            (0, north, block < deep, lats - 1, rows),
            (1, south, block + share > rows - deep, 1, -rows),
        ):
            place = deep + block + jnp.where(wanted, move, 0)
            copy = send(
                rhs.at[pl.ds(deep + block, share)], rhs.at[pl.ds(place, share)],
                fw_s.at[side, source], fw_r.at[side, source], to_lat(offset),
            )

            @pl.when(jnp.logical_and(exists, wanted))
            def _():
                if start:
                    copy.start()
                else:
                    copy.wait_send()

    forward(tm, True)
    for k, copy in enumerate(ag_sends, 1):
        copy.wait_recv()
        cross_sends.append(across(k))
        forward(block_of(pairs - k, low), True)
    for k, copy in enumerate(cross_sends):
        copy.wait_recv()
        forward(block_of(pairs - k, 1 - low), True)

    for side, arrives in ((0, south), (1, north)):
        for source in range(tms):
            block = source * share
            if (block < deep) if side == 0 else (block + share > rows - deep):
                move = rows if side == 0 else -rows
                copy = send(
                    rhs.at[pl.ds(deep + block, share)], rhs.at[pl.ds(deep + block + move, share)],
                    fw_s.at[side, source], fw_r.at[side, source], to_lat(1),
                )

                @pl.when(arrives)
                def _(copy=copy):
                    copy.wait_recv()

    def pick(source, row, code):
        a, e, w = (part[row].reshape(rank // 8, 8, WIDE) for part in source)
        code = code[None]
        moved = jnp.where(code == 1.0, e, jnp.where(code == 2.0, w, a))
        return jnp.where(code == 3.0, 0.0, moved)

    for sweep in range(SWEEPS):
        now, later = factors[sweep % 2], factors[(sweep + 1) % 2]
        least, end = sweep + 1, extent - sweep - 1

        def batch(first, now=now, later=later, sweep=sweep):
            loads = []
            for row in (first + i for i in range(BATCH)):
                sides = (now[1][row] + now[2][row]).reshape(rank // 8, 8, WIDE)
                near = sides + pick(now, row - 1, codes[row, 0]) + pick(now, row + 1, codes[row, 1])
                loads.append(rhs[row] + 0.5 * near.reshape(rank, WIDE))
            cells = split_dot(sweep_stack, jnp.concatenate(loads, axis=1))
            for i in range(BATCH):
                part = cells[:, i * WIDE : (i + 1) * WIDE]
                later[0][first + i] = part
                if sweep < SWEEPS - 1:
                    later[1][first + i] = pltpu.roll(part, WIDE - 1, 1)
                    later[2][first + i] = pltpu.roll(part, 1, 1)

        @pl.loop(0, -(-(end - least) // BATCH))
        def _(i, batch=batch, least=least, end=end):
            batch(jnp.minimum(least + BATCH * i, end - BATCH))

    last = factors[SWEEPS % 2][0]
    wide_lane = lax.broadcasted_iota(jnp.int32, (rank, WINDOW), 1)
    for row in range(rows):
        start, shift = window_of(row, points)
        cells = jnp.concatenate([last[deep + row], jnp.zeros((rank, WINDOW - WIDE), F32)], axis=1)
        if shift:
            cells = pltpu.roll(cells, shift, 1)
        inside = (wide_lane >= shift) & (wide_lane < shift + NLON)
        old = space_out[:, start : start + WINDOW]
        space_out[:, start : start + WINDOW] = jnp.where(inside, cells, old)

    for copy in [*pair_sends.values(), *rs_sends, *ag_sends, *cross_sends]:
        copy.wait_send()
    for source in range(tms):
        forward(jnp.int32(source), False)


def per_device(lats, tms, data, space_init, time_init, variable_factor, neighbours):
    var_count, hours, points = data.shape
    rank = space_init.shape[0]
    rows = points // NLON
    extent = rows + 2 * SWEEPS
    share = rows // tms
    columns = np.arange(var_count * hours)
    expand = (columns[None] // hours == np.arange(var_count)[:, None]).astype(np.float32)
    tile = (columns[None] % hours == np.arange(hours)[:, None]).astype(np.float32)
    wide = np.zeros((3 * hours, hours), np.float32)
    for h in range(hours):
        for step, tap in ((-2, 1.0), (-1, -4.0), (1, -4.0), (2, 1.0)):
            wide[hours + h + step, h] = tap
    taps = wide.reshape(3, hours, hours)
    vmem = pl.BlockSpec(memory_space=pltpu.VMEM)
    dma = pltpu.SemaphoreType.DMA
    time_factor, space_factor = pl.pallas_call(
        functools.partial(kernel, lats, tms),
        out_shape=(
            jax.ShapeDtypeStruct((hours, rank), F32),
            jax.ShapeDtypeStruct((rank, points), F32),
        ),
        in_specs=[vmem] * 8,
        out_specs=(vmem, vmem),
        scratch_shapes=[
            pltpu.VMEM((2, rank, 128), F32),
            pltpu.VMEM((lats, 2, rank, 128), F32),
            pltpu.VMEM((hours, 128), F32),
            pltpu.VMEM((2, hours, 128), F32),
            pltpu.VMEM((rank, 128), F32),
            pltpu.VMEM((tms, rank, 128), F32),
            pltpu.VMEM((rank, points), F32),
            pltpu.VMEM((rows, rank, WIDE), F32),
            pltpu.VMEM((tms, share, rank, WIDE), F32),
            pltpu.VMEM((extent, rank, WIDE), F32),
            pltpu.VMEM((extent, 2, 8, WIDE), F32),
            pltpu.VMEM((extent, rank, WIDE), F32),
            pltpu.VMEM((extent, rank, WIDE), F32),
            pltpu.VMEM((extent, rank, WIDE), F32),
            pltpu.VMEM((extent, rank, WIDE), F32),
            pltpu.VMEM((extent, rank, WIDE), F32),
            pltpu.VMEM((extent, rank, WIDE), F32),
            dma((lats,)), dma((lats,)), dma((2,)), dma((2,)), dma((2, 2)), dma((2, 2)),
            dma((tms,)), dma((tms,)), dma((tms,)), dma((tms,)), dma((tms,)), dma((tms,)),
            dma((2, tms)), dma((2, tms)),
            pltpu.VMEM((tms // 2, share, rank, WIDE), F32),
            pltpu.VMEM((tms // 2, share, rank, WIDE), F32),
            dma((tms // 2,)), dma((tms // 2,)), dma((tms // 2,)), dma((tms // 2,)),
        ],
        compiler_params=pltpu.CompilerParams(
            collective_id=0, has_side_effects=True, vmem_limit_bytes=56 * 2**20
        ),
    )(
        data.reshape(var_count * hours, points), space_init, time_init.T, variable_factor, neighbours,
        jnp.asarray(expand), jnp.asarray(tile), jnp.asarray(taps),
    )
    return time_factor.T, space_factor


def solution(mesh):
    placed = (P(None, "tm", "lat"), P(None, "lat"), P(None, "tm"), P(), P(None, "lat"))
    return jax.shard_map(
        functools.partial(per_device, mesh.shape["lat"], mesh.shape["tm"]),
        mesh=mesh,
        in_specs=placed,
        out_specs=(P(None, "tm"), P(None, "lat")),
        check_vma=False,
    )
```

```python
import functools

import jax
import jax.numpy as jnp
import numpy as np
from jax import lax
from jax.experimental import pallas as pl
from jax.experimental.pallas import tpu as pltpu
from jax.sharding import PartitionSpec as P

NLON = 360
SWEEPS = 8
WIDE = 384
SIDE = (WIDE - NLON) // 2
WINDOW = 512
BATCH = 10
F32 = jnp.float32
BF16 = jnp.bfloat16
HIGHEST = lax.Precision.HIGHEST
MESH = pl.DeviceIdType.MESH
NN = (((1,), (0,)), ((), ()))
NT = (((1,), (1,)), ((), ()))
TN = (((0,), (0,)), ((), ()))


def exact_dot(a, b, dims=NN):
    return lax.dot_general(a, b, dims, precision=HIGHEST, preferred_element_type=F32)


def halves(x):
    high = x.astype(BF16)
    return high, (x - high.astype(F32)).astype(BF16)


def left_stack(x):
    high, low = halves(x)
    return jnp.concatenate([high, high, low], axis=1)


def split_dot(stack, b):
    high, low = halves(b)
    return jnp.dot(stack, jnp.concatenate([high, low, high], axis=0), preferred_element_type=F32)


def inverse(matrix, row_id, col_id):
    for k in range(matrix.shape[0]):
        pivot = 1.0 / matrix[k : k + 1, k : k + 1]
        row = jnp.where(col_id[:1] == k, 1.0, matrix[k : k + 1, :]) * pivot
        rest = jnp.where(col_id == k, 0.0, matrix) - matrix[:, k : k + 1] * row
        matrix = jnp.where(row_id == k, row, rest)
    return matrix


def window_of(row, total):
    start = min(row * NLON // 128 * 128, total - WINDOW)
    return start, row * NLON - start


def spread_row(load, row, total, lane):
    start, shift = window_of(row, total)
    cells = load(start)
    if shift:
        cells = pltpu.roll(cells, WINDOW - shift, 1)
    cells = cells[:, :WIDE]
    after = pltpu.roll(cells, NLON, 1)
    before = pltpu.roll(cells, WIDE - NLON, 1)
    return jnp.where(lane < NLON, cells, jnp.where(lane < NLON + SIDE, after, before))


def kernel(
    lats, tms, data_ref, space_ref, time_ref, var_ref, links_ref, expand_ref, tile_ref, taps_ref,
    time_out, space_out,
    small, small_in, edge, edge_in, gram, gram_in, flat, terms, terms_in, rhs, codes,
    centre, east, west, centre_b, east_b, west_b,
    small_s, small_r, edge_s, edge_r, halo_s, halo_r, gram_s, gram_r, rs_s, rs_r, ag_s, ag_r, fw_s, fw_r,
    pair_in, partial, pair_s, pair_r, cross_s, cross_r,
):
    lat, tm = lax.axis_index("lat"), lax.axis_index("tm")
    rank, points = space_ref.shape
    hours = time_ref.shape[0]
    rows = points // NLON
    deep = SWEEPS
    extent = rows + 2 * deep
    share = rows // tms
    north, south = lat > 0, lat < lats - 1
    factors = ((centre, east, west), (centre_b, east_b, west_b))

    def to_lat(offset):
        return {"lat": lax.rem(lat + offset, lats)}

    def to_tm(offset):
        return {"tm": lax.rem(tm + offset, tms)}

    def send(src, dst, send_sem, recv_sem, device):
        return pltpu.make_async_remote_copy(
            src_ref=src, dst_ref=dst, send_sem=send_sem, recv_sem=recv_sem,
            device_id=device, device_id_type=MESH,
        )

    barrier = pltpu.get_barrier_semaphore()
    for d in range(1, lats):
        pl.semaphore_signal(barrier, inc=1, device_id=to_lat(d), device_id_type=MESH)
    for d in range(1, tms):
        pl.semaphore_signal(barrier, inc=1, device_id=to_tm(d), device_id_type=MESH)

    edge[...] = jnp.zeros_like(edge)
    edge[:, :rank] = time_ref[...]
    pl.semaphore_wait(barrier, lats + tms - 2)
    up = send(edge, edge_in.at[0], edge_s.at[0], edge_r.at[0], to_tm(1))
    down = send(edge, edge_in.at[1], edge_s.at[1], edge_r.at[1], to_tm(tms - 1))
    up.start()
    down.start()

    chunk = points // 5

    def gather(i, sums):
        cells = pl.ds(pl.multiple_of(i * chunk, 128), chunk)
        mine = space_ref[:, cells]
        return (
            sums[0] + exact_dot(mine, data_ref[:, cells], NT),
            sums[1] + exact_dot(mine, mine, NT),
        )

    projected, local_gram = lax.fori_loop(
        0, 5, gather,
        (jnp.zeros((rank, data_ref.shape[0]), F32), jnp.zeros((rank, rank), F32)),
    )
    weights = exact_dot(var_ref[...], expand_ref[...], TN)
    small[...] = jnp.zeros_like(small)
    small[0, :, :rank] = local_gram
    small[1, :, :hours] = exact_dot(projected * weights, tile_ref[...], NT)
    small_sends = []
    for d in range(1, lats):
        copy = send(small, small_in.at[d], small_s.at[d], small_r.at[d], to_lat(d))
        copy.start()
        small_sends.append(copy)

    lane = lax.broadcasted_iota(jnp.int32, (rank, WIDE), 1)
    place = lax.broadcasted_iota(jnp.int32, (1, points), 1) + lat * points
    for side, step in ((0, -NLON), (1, NLON)):
        link = links_ref[2 + side : 3 + side, :]
        shift = link - (place + step)
        ahead = (shift == 1) | (shift == 1 - NLON)
        behind = (shift == -1) | (shift == NLON - 1)
        code = jnp.where(link < 0, 3.0, jnp.where(ahead, 1.0, jnp.where(behind, 2.0, 0.0)))
        flat[0:8, :] = jnp.broadcast_to(code, (8, points))
        for row in range(rows):
            codes[deep + row, side] = spread_row(
                lambda s: flat[0:8, s : s + WINDOW], row, points, lane[:8]
            )
    for row in range(rows):
        centre[deep + row] = spread_row(
            lambda s: space_ref[:, s : s + WINDOW], row, points, lane
        )
    top, bottom = pl.ds(deep, deep), pl.ds(rows, deep)
    before, behind_rows = pl.ds(0, deep), pl.ds(rows + deep, deep)
    halo = []
    for side, (exists, mine, theirs, offset) in enumerate(
        ((north, top, behind_rows, lats - 1), (south, bottom, before, 1))
    ):
        a = send(centre.at[mine], centre.at[theirs], halo_s.at[side, 0], halo_r.at[side, 0], to_lat(offset))
        b = send(codes.at[mine], codes.at[theirs], halo_s.at[side, 1], halo_r.at[side, 1], to_lat(offset))
        halo.append((exists, a, b))

        @pl.when(exists)
        def _(a=a, b=b):
            a.start()
            b.start()

    row_id = lax.broadcasted_iota(jnp.int32, (rank, rank), 0)
    col_id = lax.broadcasted_iota(jnp.int32, (rank, rank), 1)
    eye = jnp.where(row_id == col_id, F32(1.0), F32(0.0))
    var_gram = exact_dot(var_ref[...], var_ref[...], TN)
    up.wait()
    down.wait()
    past = jnp.where(tm > 0, edge_in[0, :, :rank], 0.0)
    coming = jnp.where(tm < tms - 1, edge_in[1, :, :rank], 0.0)
    stencil = (
        exact_dot(past, taps_ref[0], TN)
        + exact_dot(time_ref[...], taps_ref[1], TN)
        + exact_dot(coming, taps_ref[2], TN)
    )
    total = small[...]
    for d, copy in enumerate(small_sends, 1):
        copy.wait()
        total = total + small_in[d]
    space_gram, time_rhs = total[0, :, :rank], total[1, :, :hours]
    time_inv = inverse(space_gram * var_gram + 3.0 * eye, row_id, col_id)
    time_factor = exact_dot(time_inv, time_rhs - 0.5 * stencil)
    time_out[...] = exact_dot(time_factor, eye, TN)
    gram[...] = jnp.zeros_like(gram)
    gram[:, :rank] = exact_dot(time_factor, time_factor, NT)
    gram_sends = []
    for d in range(1, tms):
        copy = send(gram, gram_in.at[d], gram_s.at[d], gram_r.at[d], to_tm(d))
        copy.start()
        gram_sends.append(copy)

    stack = left_stack(weights * exact_dot(time_factor, tile_ref[...]))

    @pl.loop(0, 5)
    def _(i):
        cells = pl.ds(pl.multiple_of(i * chunk, 128), chunk)
        flat[:, cells] = split_dot(stack, data_ref[:, cells])

    for row in range(rows):
        terms[row] = spread_row(lambda s: flat[:, s : s + WINDOW], row, points, lane)
    pairs = tms // 2
    low = lax.rem(tm, 2)
    other = {"tm": tm + 1 - 2 * low}

    def block_of(k, side):
        return lax.rem(tm // 2 + k, pairs) * 2 + side

    order = [*range(1, pairs), 0]
    pair_sends = {}
    for k in order:
        block = pl.ds(block_of(k, 1 - low) * share, share)
        pair_sends[k] = send(terms.at[block], pair_in.at[k], pair_s.at[k], pair_r.at[k], other)
        pair_sends[k].start()
    rs_sends = []
    for k in range(1, pairs):
        pair_sends[k].wait_recv()
        partial[k] = terms[pl.ds(block_of(k, low) * share, share)] + pair_in[k]
        copy = send(partial.at[k], terms_in.at[k], rs_s.at[k], rs_r.at[k], to_tm(2 * k))
        copy.start()
        rs_sends.append(copy)

    time_gram = gram[:, :rank]
    for d, copy in enumerate(gram_sends, 1):
        copy.wait()
        time_gram = time_gram + gram_in[d, :, :rank]
    diagonal = time_gram * eye
    scale = jnp.sqrt(jnp.sum(diagonal, axis=1, keepdims=True) + 1e-06)
    scale_row = jnp.sqrt(jnp.sum(diagonal, axis=0, keepdims=True) + 1e-06)
    point_inv = inverse(time_gram / (scale * scale_row) * var_gram + 2.0 * eye, row_id, col_id)
    sweep_stack = left_stack(point_inv)

    mine = pl.ds(tm * share, share)
    pair_sends[0].wait_recv()
    owned = terms[mine] + pair_in[0]
    for d, copy in enumerate(rs_sends, 1):
        copy.wait_recv()
        owned = owned + terms_in[d]
    held = pl.ds(deep + tm * share, share)
    rhs[held] = owned / scale[None]
    ag_sends = []
    for k in range(1, pairs):
        copy = send(rhs.at[held], rhs.at[held], ag_s.at[k], ag_r.at[k], to_tm(2 * k))
        copy.start()
        ag_sends.append(copy)

    def across(k):
        block = pl.ds(deep + block_of(pairs - k, low) * share, share)
        copy = send(rhs.at[block], rhs.at[block], cross_s.at[k], cross_r.at[k], other)
        copy.start()
        return copy

    cross_sends = [across(0)]

    for side, arrives in ((0, south), (1, north)):
        _, a, b = halo[side]

        @pl.when(arrives)
        def _(a=a, b=b):
            a.wait_recv()
            b.wait_recv()

    for exists, a, b in halo:

        @pl.when(exists)
        def _(a=a, b=b):
            a.wait_send()
            b.wait_send()

    @pl.loop(0, extent)
    def _(row):
        cells = centre[row]
        east[row] = pltpu.roll(cells, WIDE - 1, 1)
        west[row] = pltpu.roll(cells, 1, 1)

    def forward(source, start):
        block = source * share
        for side, exists, wanted, offset, move in (
            (0, north, block < deep, lats - 1, rows),
            (1, south, block + share > rows - deep, 1, -rows),
        ):
            place = deep + block + jnp.where(wanted, move, 0)
            copy = send(
                rhs.at[pl.ds(deep + block, share)], rhs.at[pl.ds(place, share)],
                fw_s.at[side, source], fw_r.at[side, source], to_lat(offset),
            )

            @pl.when(jnp.logical_and(exists, wanted))
            def _():
                if start:
                    copy.start()
                else:
                    copy.wait_send()

    forward(tm, True)
    for k, copy in enumerate(ag_sends, 1):
        copy.wait_recv()
        cross_sends.append(across(k))
        forward(block_of(pairs - k, low), True)
    for k, copy in enumerate(cross_sends):
        copy.wait_recv()
        forward(block_of(pairs - k, 1 - low), True)

    for side, arrives in ((0, south), (1, north)):
        for source in range(tms):
            block = source * share
            if (block < deep) if side == 0 else (block + share > rows - deep):
                move = rows if side == 0 else -rows
                copy = send(
                    rhs.at[pl.ds(deep + block, share)], rhs.at[pl.ds(deep + block + move, share)],
                    fw_s.at[side, source], fw_r.at[side, source], to_lat(1),
                )

                @pl.when(arrives)
                def _(copy=copy):
                    copy.wait_recv()

    def pick(source, row, code):
        a, e, w = (part[row].reshape(rank // 8, 8, WIDE) for part in source)
        code = code[None]
        moved = jnp.where(code == 1.0, e, jnp.where(code == 2.0, w, a))
        return jnp.where(code == 3.0, 0.0, moved)

    for sweep in range(SWEEPS):
        now, later = factors[sweep % 2], factors[(sweep + 1) % 2]
        least, end = sweep + 1, extent - sweep - 1
        steps = -(-(end - least) // BATCH)
        size = -(-(end - least) // steps)

        def batch(first, now=now, later=later, sweep=sweep, size=size):
            loads = []
            for row in (first + i for i in range(size)):
                sides = (now[1][row] + now[2][row]).reshape(rank // 8, 8, WIDE)
                near = sides + pick(now, row - 1, codes[row, 0]) + pick(now, row + 1, codes[row, 1])
                loads.append(rhs[row] + 0.5 * near.reshape(rank, WIDE))
            cells = split_dot(sweep_stack, jnp.concatenate(loads, axis=1))
            for i in range(size):
                part = cells[:, i * WIDE : (i + 1) * WIDE]
                later[0][first + i] = part
                if sweep < SWEEPS - 1:
                    later[1][first + i] = pltpu.roll(part, WIDE - 1, 1)
                    later[2][first + i] = pltpu.roll(part, 1, 1)

        @pl.loop(0, steps)
        def _(i, batch=batch, least=least, end=end, size=size):
            batch(jnp.minimum(least + size * i, end - size))

    last = factors[SWEEPS % 2][0]
    wide_lane = lax.broadcasted_iota(jnp.int32, (rank, WINDOW), 1)
    for row in range(rows):
        start, shift = window_of(row, points)
        cells = jnp.concatenate([last[deep + row], jnp.zeros((rank, WINDOW - WIDE), F32)], axis=1)
        if shift:
            cells = pltpu.roll(cells, shift, 1)
        inside = (wide_lane >= shift) & (wide_lane < shift + NLON)
        old = space_out[:, start : start + WINDOW]
        space_out[:, start : start + WINDOW] = jnp.where(inside, cells, old)

    for copy in [*pair_sends.values(), *rs_sends, *ag_sends, *cross_sends]:
        copy.wait_send()
    for source in range(tms):
        forward(jnp.int32(source), False)


def per_device(lats, tms, data, space_init, time_init, variable_factor, neighbours):
    var_count, hours, points = data.shape
    rank = space_init.shape[0]
    rows = points // NLON
    extent = rows + 2 * SWEEPS
    share = rows // tms
    columns = np.arange(var_count * hours)
    expand = (columns[None] // hours == np.arange(var_count)[:, None]).astype(np.float32)
    tile = (columns[None] % hours == np.arange(hours)[:, None]).astype(np.float32)
    wide = np.zeros((3 * hours, hours), np.float32)
    for h in range(hours):
        for step, tap in ((-2, 1.0), (-1, -4.0), (1, -4.0), (2, 1.0)):
            wide[hours + h + step, h] = tap
    taps = wide.reshape(3, hours, hours)
    vmem = pl.BlockSpec(memory_space=pltpu.VMEM)
    dma = pltpu.SemaphoreType.DMA
    time_factor, space_factor = pl.pallas_call(
        functools.partial(kernel, lats, tms),
        out_shape=(
            jax.ShapeDtypeStruct((hours, rank), F32),
            jax.ShapeDtypeStruct((rank, points), F32),
        ),
        in_specs=[vmem] * 8,
        out_specs=(vmem, vmem),
        scratch_shapes=[
            pltpu.VMEM((2, rank, 128), F32),
            pltpu.VMEM((lats, 2, rank, 128), F32),
            pltpu.VMEM((hours, 128), F32),
            pltpu.VMEM((2, hours, 128), F32),
            pltpu.VMEM((rank, 128), F32),
            pltpu.VMEM((tms, rank, 128), F32),
            pltpu.VMEM((rank, points), F32),
            pltpu.VMEM((rows, rank, WIDE), F32),
            pltpu.VMEM((tms, share, rank, WIDE), F32),
            pltpu.VMEM((extent, rank, WIDE), F32),
            pltpu.VMEM((extent, 2, 8, WIDE), F32),
            pltpu.VMEM((extent, rank, WIDE), F32),
            pltpu.VMEM((extent, rank, WIDE), F32),
            pltpu.VMEM((extent, rank, WIDE), F32),
            pltpu.VMEM((extent, rank, WIDE), F32),
            pltpu.VMEM((extent, rank, WIDE), F32),
            pltpu.VMEM((extent, rank, WIDE), F32),
            dma((lats,)), dma((lats,)), dma((2,)), dma((2,)), dma((2, 2)), dma((2, 2)),
            dma((tms,)), dma((tms,)), dma((tms,)), dma((tms,)), dma((tms,)), dma((tms,)),
            dma((2, tms)), dma((2, tms)),
            pltpu.VMEM((tms // 2, share, rank, WIDE), F32),
            pltpu.VMEM((tms // 2, share, rank, WIDE), F32),
            dma((tms // 2,)), dma((tms // 2,)), dma((tms // 2,)), dma((tms // 2,)),
        ],
        compiler_params=pltpu.CompilerParams(
            collective_id=0, has_side_effects=True, vmem_limit_bytes=56 * 2**20
        ),
    )(
        data.reshape(var_count * hours, points), space_init, time_init.T, variable_factor, neighbours,
        jnp.asarray(expand), jnp.asarray(tile), jnp.asarray(taps),
    )
    return time_factor.T, space_factor


def solution(mesh):
    placed = (P(None, "tm", "lat"), P(None, "lat"), P(None, "tm"), P(), P(None, "lat"))
    return jax.shard_map(
        functools.partial(per_device, mesh.shape["lat"], mesh.shape["tm"]),
        mesh=mesh,
        in_specs=placed,
        out_specs=(P(None, "tm"), P(None, "lat")),
        check_vma=False,
    )
```
